32 devices in a mesh: dp: 4 (over x, core), expert: 8 (over z, y).
Axes of the slice: x: 2, y: 2, z: 4, core: 2. Of those that a mesh axis runs over, the one named last changes fastest.
Arguments:
- tokens: bfloat16 [4096, 2048], P(('dp', 'expert')), may hold values from -6 to 6
- grad_out: bfloat16 [4096, 2048], P(('dp', 'expert')), may hold values from -6 to 6
- routes: int32 [4096, 6], P(('dp', 'expert')), may hold values from 0 to 15, all different within a row; in each aligned block of 128 rows (0 to 127, 128 to 255, ...) at most 72 rows name the same one
- combine: bfloat16 [4096, 6], P(('dp', 'expert')), may hold values from 0.099609375 to 1
- w_gate: bfloat16 [16, 2048, 704], P('expert'), may hold values from -0.125 to 0.125
- w_up: bfloat16 [16, 2048, 704], P('expert'), may hold values from -0.125 to 0.125
- w_down: bfloat16 [16, 704, 2048], P('expert'), may hold values from -0.21875 to 0.21875
Outputs:
- grad_tokens: bfloat16 [4096, 2048], P(('dp', 'expert'))
- grad_combine: bfloat16 [4096, 6], P(('dp', 'expert'))
- grad_gate: bfloat16 [16, 2048, 704], P('expert', 'dp')
- grad_up: bfloat16 [16, 2048, 704], P('expert', 'dp')
- grad_down: bfloat16 [16, 704, 2048], P('expert', None, 'dp')
The draws below stay inside these ranges and needn't reach their ends.
Inputs may be any that keep to these rules, and one draw needn't show every extreme that they name: `routes`: each row names 6 different experts. Among the rows of one device no expert is named more than 72 times, a bound that some block reaches.
All inputs are finite; a program needn't handle non-finite values.
Results may differ from the reference program's by a relative error of at most 0.009.
Values may be sent and summed in bfloat16 or wider, within the bound.
A program may use at most 192 MiB of HBM per device.

```python
import math
import jax
import jax.numpy as jnp
import numpy as np
from jax import lax

D = 2048
H = 704
TOPK = 6
TOK_DEV = 128
EXPERTS = 16
CAP = 72
TOKENS = 4096
N_DP = 4
N_EXPERT = 8


def raised(values, stream_key, source, target, blocks, factor):
    owner, partner = [(jnp.arange(values.shape[dim]) // (values.shape[dim] // blocks)).reshape([-1 if axis == dim else 1 for axis in range(values.ndim)]) for dim in (source, target)]
    chosen = jax.random.permutation(stream_key, blocks)[partner]
    strong = (owner == chosen) | (owner == (partner + blocks // 2) % blocks)
    return jnp.where(strong, factor * values, values)


def levels(key, shape, shards, low, top_value):
    loudness, own = 1.0, jax.random.fold_in(key, 6)
    for axis_at, blocks in shards:
        steps = jnp.exp(jax.random.uniform(jax.random.fold_in(own, axis_at), (blocks,), jnp.float32, low / len(shards), top_value / len(shards)))
        loudness = loudness * jnp.repeat(steps, shape[axis_at] // blocks).reshape([-1 if axis == axis_at else 1 for axis in range(len(shape))])
    return loudness


def deal_out(own_key, own, number, rows, count, top, most, slope):
    order = jax.random.permutation(own_key, count)
    packed, usual = load_shares(count, rows * top, most, slope, True), load_shares(count, rows * top, most, slope, False)
    places = jnp.arange(count)

    def named(sizes, turn):
        used = int((sizes > 0).sum())
        fixed = max(1, used // 4)
        passed = fixed + (places - fixed + turn * (used - fixed)) % max(1, count - fixed)
        return jnp.zeros((count,), jnp.int32).at[order[jnp.where(places < fixed, places, passed)]].set(jnp.asarray(sizes, jnp.int32))

    sizes = jnp.where(number % 4 == 0, named(packed, number // 4), named(usual, number - number // 4 - 1))
    mixed = jax.random.permutation(jax.random.fold_in(own, 3), count)
    donor, taker = mixed[0:count // 2 * 2:2], mixed[1:count // 2 * 2:2]
    room = jnp.minimum(sizes[donor] - 1, most - sizes[taker]) // 2
    room = jnp.where((donor == order[0]) | (taker == order[0]) | (sizes[taker] == 0), 0, jnp.maximum(room, 0))
    passed = jax.random.randint(jax.random.fold_in(own, 4), (count // 2,), 0, 1 << 20) % (room + 1)
    sizes = sizes.at[donor].add(-passed).at[taker].add(passed)
    items = jnp.searchsorted(jnp.cumsum(sizes), jnp.arange(rows * top), side="right").astype(jnp.int32)
    listing = items.reshape(top, rows).T
    listing = listing[jax.random.permutation(jax.random.fold_in(own, 1), rows)]
    turn = jax.random.randint(jax.random.fold_in(own, 2), (rows, 1), 0, top)
    return jnp.take_along_axis(listing, (jnp.arange(top)[None, :] + turn) % top, axis=1)


def load_shares(count, total, reach, skew, full):
    loads = [(1 << 20) // math.isqrt(grade ** skew) + 1 for grade in range(1, count + 1)]
    largest = reach if full else min(reach, max(-(-total // count), total * loads[0] // sum(loads)))
    least = 1 if total - largest >= count - 1 else 0
    holding, spare = [largest] + [least] * (count - 1), total - largest - least * (count - 1)
    while spare > 0:
        candidates = [i for i in range(1, count) if holding[i] < largest] or [i for i in range(1, count) if holding[i] < reach]
        pool, left = sum([loads[i] for i in candidates]), spare
        for i in candidates:
            extra = min(reach - holding[i], max(1, left * loads[i] // pool), spare)
            holding[i] = holding[i] + extra
            spare = spare - extra
    return np.array(holding)


def normal_values(own_key, extent, spread, bound, cuts=(), kind=jnp.bfloat16):
    array = spread * jax.random.normal(own_key, extent, jnp.float32)
    if cuts:
        array = array * levels(own_key, extent, cuts, -0.22, 0.18)
    return jnp.clip(array, -bound, bound).astype(kind)


def noise_with(stream_key, extent, spread, bound, cuts, heavy, kind=jnp.bfloat16):
    drawn = spread * jax.random.normal(stream_key, extent, jnp.float32)
    if cuts:
        drawn = drawn * levels(stream_key, extent, cuts, -0.22, 0.18)
    return jnp.clip(raised(drawn, jax.random.fold_in(stream_key, 3), *heavy), -bound, bound).astype(kind)


def setup_inputs(seed: int = 0) -> dict:
    seeds = jax.random.split(jax.random.key(seed), 8)
    tokens = noise_with(seeds[0], (TOKENS, D), 1.0, 6.0, ((0, 32),), (0, 1, 32, 2.75))
    grad_out = noise_with(seeds[1], (TOKENS, D), 1.0, 6.0, ((0, 32),), (0, 1, 32, 2.75))
    routes_keys = jax.random.split(jax.random.fold_in(seeds[2], 1), TOKENS // TOK_DEV)
    routes_turns = jax.random.permutation(jax.random.fold_in(seeds[2], 3), TOKENS // TOK_DEV)
    routes = jax.vmap(lambda own, number: deal_out(jax.random.fold_in(seeds[2], 2), own, number, TOK_DEV, EXPERTS, TOPK, CAP, 2))(routes_keys, routes_turns).reshape((TOKENS, TOPK))
    combine = jnp.clip(jnp.exp(math.log(1.0) - 2.306499 * jax.random.uniform(seeds[3], (TOKENS, TOPK), jnp.float32) ** levels(seeds[3], (TOKENS, TOPK), ((0, 32),), -0.2, 0.2)), 0.099609375, 1.0).astype(jnp.bfloat16)
    w_gate = normal_values(seeds[4], (EXPERTS, D, H), D ** -0.5, 0.125, ((0, 8),))
    w_up = normal_values(seeds[5], (EXPERTS, D, H), D ** -0.5, 0.125, ((0, 8),))
    w_down = normal_values(seeds[6], (EXPERTS, H, D), H ** -0.5, 0.21875, ((0, 8),))
    return {"tokens": tokens, "grad_out": grad_out, "routes": routes, "combine": combine, "w_gate": w_gate, "w_up": w_up, "w_down": w_down}


def slot_tables(routes, experts, capacity):
    tok_count, top_count = routes.shape
    slot_count = tok_count * top_count
    flat_routes = routes.reshape(-1)
    one_hot = (flat_routes[:, None] == jnp.arange(experts, dtype=jnp.int32)[None, :]).astype(jnp.int32)
    position = jnp.sum((jnp.cumsum(one_hot, axis=0) - 1) * one_hot, axis=1)
    target = (flat_routes * capacity + position).astype(jnp.int32)
    slot_table = jnp.full((experts * capacity,), slot_count, jnp.int32)
    slot_table = slot_table.at[target].set(jnp.arange(slot_count, dtype=jnp.int32))
    return slot_table, target


def expert_forward(rows_x, gate_weights, up_weights, down_weights):
    pre_gate = jnp.dot(rows_x, gate_weights, preferred_element_type=jnp.float32)
    pre_up = jnp.dot(rows_x, up_weights, preferred_element_type=jnp.float32)
    sigma = jax.nn.sigmoid(pre_gate)
    hidden = (pre_gate * sigma * pre_up).astype(jnp.bfloat16)
    output = jnp.dot(hidden, down_weights, preferred_element_type=jnp.float32)
    return pre_gate, pre_up, sigma, hidden, output


def expert_backward(rows_dy, rows_weight, state, gate_weights, up_weights, down_weights):
    pre_gate, pre_up, sigma, hidden, output = state
    grad_weight = jnp.sum(rows_dy.astype(jnp.float32) * output, axis=-1).astype(jnp.bfloat16)
    scaled = (rows_weight.astype(jnp.float32)[:, None] * rows_dy.astype(jnp.float32)).astype(jnp.bfloat16)
    grad_hidden = jnp.dot(scaled, down_weights.T, preferred_element_type=jnp.float32)
    grad_gate = (grad_hidden * pre_up * sigma * (1.0 + pre_gate * (1.0 - sigma))).astype(jnp.bfloat16)
    grad_up = (grad_hidden * pre_gate * sigma).astype(jnp.bfloat16)
    grad_rows = (jnp.dot(grad_gate, gate_weights.T, preferred_element_type=jnp.float32)
                 + jnp.dot(grad_up, up_weights.T, preferred_element_type=jnp.float32)).astype(jnp.bfloat16)
    return grad_rows, grad_weight, grad_gate, grad_up, scaled


def weight_terms(rows_x, grad_gate, grad_up, scaled, hidden):
    gate_term = jnp.dot(rows_x.T, grad_gate, preferred_element_type=jnp.float32)
    up_term = jnp.dot(rows_x.T, grad_up, preferred_element_type=jnp.float32)
    down_term = jnp.dot(hidden.T, scaled, preferred_element_type=jnp.float32)
    return gate_term, up_term, down_term


def replica_total(parts):
    rounded = lax.optimization_barrier(parts.astype(jnp.bfloat16))
    return jnp.sum(rounded.astype(jnp.float32), axis=0).astype(jnp.bfloat16)


def reference(tokens, grad_out, routes, combine, w_gate, w_up, w_down):
    blocks = N_DP * N_EXPERT
    slot_count = TOK_DEV * TOPK
    tables, targets = jax.vmap(lambda block_routes: slot_tables(block_routes, EXPERTS, CAP))(
        routes.reshape(blocks, TOK_DEV, TOPK))
    token_index = jnp.where(tables < slot_count, tables // TOPK, TOK_DEV).astype(jnp.int32)
    x_padded = jnp.concatenate([tokens.reshape(blocks, TOK_DEV, D), jnp.zeros((blocks, 1, D), jnp.bfloat16)], axis=1)
    dy_padded = jnp.concatenate([grad_out.reshape(blocks, TOK_DEV, D), jnp.zeros((blocks, 1, D), jnp.bfloat16)], axis=1)
    weight_padded = jnp.concatenate([combine.reshape(blocks, slot_count), jnp.zeros((blocks, 1), jnp.bfloat16)], axis=1)

    def pick_rows(source, index):
        return source[index]

    def per_expert(operands):
        expert_id, gate_weights, up_weights, down_weights = operands
        index = lax.dynamic_slice_in_dim(token_index, (expert_id * CAP).astype(jnp.int32), CAP, 1)
        slot_index = lax.dynamic_slice_in_dim(tables, (expert_id * CAP).astype(jnp.int32), CAP, 1)
        rows_x = jax.vmap(pick_rows)(x_padded, index).reshape(N_DP, N_EXPERT * CAP, D)
        rows_dy = jax.vmap(pick_rows)(dy_padded, index).reshape(N_DP, N_EXPERT * CAP, D)
        rows_weight = jax.vmap(pick_rows)(weight_padded, slot_index).reshape(N_DP, N_EXPERT * CAP)
        state = jax.vmap(expert_forward, in_axes=(0, None, None, None))(rows_x, gate_weights, up_weights, down_weights)
        grad_rows, grad_weight, grad_gate, grad_up, scaled = jax.vmap(
            expert_backward, in_axes=(0, 0, 0, None, None, None))(rows_dy, rows_weight, state, gate_weights, up_weights, down_weights)
        gate_term, up_term, down_term = jax.vmap(weight_terms)(rows_x, grad_gate, grad_up, scaled, state[3])
        return (grad_rows.reshape(blocks, CAP, D), grad_weight.reshape(blocks, CAP),
                replica_total(gate_term), replica_total(up_term), replica_total(down_term))

    grad_rows, grad_weight, grad_gate, grad_up, grad_down = lax.map(
        per_expert, (jnp.arange(EXPERTS, dtype=jnp.int32), w_gate, w_up, w_down))
    grad_rows = jnp.transpose(grad_rows, (1, 0, 2, 3)).reshape(blocks, EXPERTS * CAP, D)
    grad_weight = jnp.transpose(grad_weight, (1, 0, 2)).reshape(blocks, EXPERTS * CAP)
    picked = jax.vmap(pick_rows)(grad_rows, targets).reshape(blocks, TOK_DEV, TOPK, D)
    grad_tokens = jnp.sum(picked.astype(jnp.float32), axis=2).astype(jnp.bfloat16).reshape(TOKENS, D)
    grad_combine = jax.vmap(pick_rows)(grad_weight, targets).reshape(TOKENS, TOPK)
    return grad_tokens, grad_combine, grad_gate, grad_up, grad_down
```

```python
import jax
import jax.numpy as jnp
from jax import lax
from jax.sharding import PartitionSpec as P

F32 = jnp.float32
BF16 = jnp.bfloat16
LANES = 128


def dot(left, right):
    return jnp.dot(left, right, preferred_element_type=F32)


def dot_ta(left, right):
    return lax.dot_general(left, right, (((0,), (0,)), ((), ())), preferred_element_type=F32)


def dot_tb(left, right):
    return lax.dot_general(left, right, (((1,), (1,)), ((), ())), preferred_element_type=F32)


def replica_scatter(make_part, count, axis):
    if count == 1 or count & (count - 1):
        raise ValueError("dp size")
    me = lax.axis_index("dp")
    low = me & 1
    send = make_part(1 - low).astype(BF16)
    got = lax.ppermute(send, "dp", [(i, i ^ 1) for i in range(count)])
    total = make_part(low) + got.astype(F32)
    bit = 2
    while bit < count:
        size = total.shape[axis] // (count // bit)
        halves = count // bit // 2
        shape = total.shape
        split = total.reshape(shape[:axis] + (halves, 2, size) + shape[axis + 1 :])
        side = (me // bit) & 1
        other = lax.dynamic_index_in_dim(split, 1 - side, axis + 1, keepdims=False)
        mine = lax.dynamic_index_in_dim(split, side, axis + 1, keepdims=False)
        flat = shape[:axis] + (halves * size,) + shape[axis + 1 :]
        got = lax.ppermute(
            other.reshape(flat).astype(BF16), "dp", [(i, i ^ bit) for i in range(count)]
        )
        total = mine.reshape(flat) + got.astype(F32)
        bit *= 2
    return total.astype(BF16)


def columns(array, count, low):
    rows, width = array.shape
    size = width // count
    split = array.reshape(rows, count // 2, 2, size)
    return lax.dynamic_index_in_dim(split, low, 2, keepdims=False).reshape(rows, width // 2)


def shards(tokens, grad_out, routes, combine, w_gate, w_up, w_down):
    tok_count, width = tokens.shape
    top_count = routes.shape[1]
    exp_local = w_gate.shape[0]
    owners = lax.axis_size("expert")
    replicas = lax.axis_size("dp")
    experts = exp_local * owners
    capacity = min(tok_count, 3 * tok_count * top_count // (2 * experts))
    slots = owners * capacity
    all_count = owners * tok_count
    me = lax.axis_index("expert")

    named = routes[:, :, None] == jnp.arange(experts, dtype=jnp.int32)[None, None, :]
    dense_weight = jnp.sum(jnp.where(named, combine.astype(F32)[:, :, None], 0.0), axis=1)
    dense_named = jnp.sum(named.astype(F32), axis=1)
    meta = jnp.concatenate([dense_named, dense_weight], axis=1).astype(BF16)

    all_meta = lax.all_gather(meta, "expert", axis=0, tiled=True)
    all_x = lax.all_gather(tokens, "expert", axis=0, tiled=True)
    all_dy = lax.all_gather(grad_out, "expert", axis=0, tiled=True)

    first = me * exp_local
    mask = lax.dynamic_slice_in_dim(all_meta, first, exp_local, 1).astype(F32).T
    weight = lax.dynamic_slice_in_dim(all_meta, experts + first, exp_local, 1)
    position = jnp.cumsum(mask, axis=1).astype(jnp.int32) - 1
    position = jnp.where(mask > 0.5, position, -1)

    token_parts = jnp.zeros((all_count, width), F32)
    combine_parts = []
    gates, ups, downs = [], [], []
    for local in range(exp_local):
        pick = (
            position[local][None, :] == jnp.arange(slots, dtype=jnp.int32)[:, None]
        ).astype(BF16)
        rows_x = dot(pick, all_x).astype(BF16)
        pre_gate = dot(rows_x, w_gate[local])
        pre_up = dot(rows_x, w_up[local])
        sigma = jax.nn.sigmoid(pre_gate)
        hidden = (pre_gate * sigma * pre_up).astype(BF16)
        rows_dy = dot(pick, all_dy).astype(BF16)
        rows_weight = dot(pick, weight[:, local : local + 1])
        scaled = (rows_weight * rows_dy.astype(F32)).astype(BF16)
        grad_hidden = dot_tb(scaled, w_down[local])
        grad_gate = (grad_hidden * pre_up * sigma * (1.0 + pre_gate * (1.0 - sigma))).astype(BF16)
        grad_up = (grad_hidden * pre_gate * sigma).astype(BF16)
        gates.append(
            replica_scatter(
                lambda low: dot_ta(columns(rows_x, replicas, low), grad_gate), replicas, 0
            )
        )
        ups.append(
            replica_scatter(
                lambda low: dot_ta(columns(rows_x, replicas, low), grad_up), replicas, 0
            )
        )
        downs.append(
            replica_scatter(
                lambda low: dot_ta(hidden, columns(scaled, replicas, low)), replicas, 1
            )
        )
        grad_rows = (dot_tb(grad_gate, w_gate[local]) + dot_tb(grad_up, w_up[local])).astype(BF16)
        token_parts = token_parts + dot_ta(pick, grad_rows)
        output = dot(hidden, w_down[local])
        grad_weight = jnp.sum(rows_dy.astype(F32) * output, axis=-1, keepdims=True).astype(BF16)
        combine_parts.append(dot_ta(pick, grad_weight))
    spread = jnp.concatenate(combine_parts, axis=1).astype(BF16)
    spread = lax.all_to_all(
        spread.reshape(owners, tok_count, exp_local), "expert", 0, 0, tiled=True
    )
    spread = spread.transpose(1, 0, 2).reshape(tok_count, experts).astype(F32)
    grad_tokens = lax.psum_scatter(
        token_parts.astype(BF16), "expert", scatter_dimension=0, tiled=True
    )
    grad_combine = jnp.sum(jnp.where(named, spread[:, None, :], 0.0), axis=2).astype(BF16)
    return (grad_tokens, grad_combine, jnp.stack(gates), jnp.stack(ups), jnp.stack(downs))


def solution(mesh):
    return jax.shard_map(
        shards,
        mesh=mesh,
        in_specs=(
            P(("dp", "expert"), None),
            P(("dp", "expert"), None),
            P(("dp", "expert"), None),
            P(("dp", "expert"), None),
            P("expert", None, None),
            P("expert", None, None),
            P("expert", None, None),
        ),
        out_specs=(
            P(("dp", "expert"), None),
            P(("dp", "expert"), None),
            P("expert", "dp", None),
            P("expert", "dp", None),
            P("expert", None, "dp"),
        ),
        check_vma=False,
    )
```

```python
import functools

import jax
import jax.numpy as jnp
from jax import lax
from jax.experimental import pallas as pl
from jax.experimental.pallas import tpu as pltpu
from jax.sharding import PartitionSpec as P

F32 = jnp.float32
BF16 = jnp.bfloat16
LANES = 128
MESH = pl.DeviceIdType.MESH


def dot(left, right):
    return jnp.dot(left, right, preferred_element_type=F32)


def dot_ta(left, right):
    return lax.dot_general(left, right, (((0,), (0,)), ((), ())), preferred_element_type=F32)


def dot_tb(left, right):
    return lax.dot_general(left, right, (((1,), (1,)), ((), ())), preferred_element_type=F32)


def gather_kernel(lines, x_ref, m_ref, ox_ref, om_ref, own, send_z, recv_z, send_y, recv_y):
    me = lax.axis_index("expert")
    line, side = me // 2, lax.rem(me, 2)
    across = line * 2 + 1 - side

    def peer(step):
        return lax.rem(line + step, lines) * 2 + side

    barrier = pltpu.get_barrier_semaphore()
    for step in range(1, lines):
        pl.semaphore_signal(barrier, inc=1, device_id={"expert": peer(step)}, device_id_type=MESH)
    pl.semaphore_signal(barrier, inc=1, device_id={"expert": across}, device_id_type=MESH)
    pl.semaphore_wait(barrier, lines)

    arrays = ((0, m_ref, om_ref), (1, x_ref, ox_ref))
    locals_, sends = [], []
    for which, src, dst in arrays:
        copy = pltpu.make_async_copy(src, dst.at[me], own.at[which])
        copy.start()
        locals_.append(copy)
        for step in range(1, lines):
            copy = pltpu.make_async_remote_copy(
                src_ref=src,
                dst_ref=dst.at[me],
                send_sem=send_z.at[which, step - 1],
                recv_sem=recv_z.at[which, step - 1],
                device_id={"expert": peer(step)},
                device_id_type=MESH,
            )
            copy.start()
            sends.append(copy)
        copy = pltpu.make_async_remote_copy(
            src_ref=src,
            dst_ref=dst.at[me],
            send_sem=send_y.at[which, 0],
            recv_sem=recv_y.at[which, 0],
            device_id={"expert": across},
            device_id_type=MESH,
        )
        copy.start()
        sends.append(copy)
    for which, src, dst in arrays:
        for step in sorted(range(1, lines), key=lambda s: min(s, lines - s)):
            origin = peer(lines - step)
            pltpu.make_async_remote_copy(
                src_ref=src,
                dst_ref=dst.at[origin],
                send_sem=send_z.at[which, step - 1],
                recv_sem=recv_z.at[which, step - 1],
                device_id={"expert": across},
                device_id_type=MESH,
            ).wait_recv()
            copy = pltpu.make_async_remote_copy(
                src_ref=dst.at[origin],
                dst_ref=dst.at[origin],
                send_sem=send_y.at[which, step],
                recv_sem=recv_y.at[which, step],
                device_id={"expert": across},
                device_id_type=MESH,
            )
            copy.start()
            sends.append(copy)
    for copy in locals_:
        copy.wait()
    for copy in sends:
        copy.wait_send()
    for which, src, dst in arrays:
        for step in range(lines):
            origin = lax.rem(line + lines - step, lines) * 2 + 1 - side
            pltpu.make_async_remote_copy(
                src_ref=src,
                dst_ref=dst.at[origin],
                send_sem=send_y.at[which, step],
                recv_sem=recv_y.at[which, step],
                device_id={"expert": across},
                device_id_type=MESH,
            ).wait_recv()


def gather_pair(tokens, meta, owners):
    lines = owners // 2
    anywhere = pl.BlockSpec(memory_space=pl.ANY)
    return pl.pallas_call(
        functools.partial(gather_kernel, lines),
        out_shape=(
            jax.ShapeDtypeStruct((owners,) + tokens.shape, tokens.dtype),
            jax.ShapeDtypeStruct((owners,) + meta.shape, meta.dtype),
        ),
        in_specs=[anywhere, anywhere],
        out_specs=(anywhere, anywhere),
        scratch_shapes=[
            pltpu.SemaphoreType.DMA((2,)),
            pltpu.SemaphoreType.DMA((2, lines - 1)),
            pltpu.SemaphoreType.DMA((2, lines - 1)),
            pltpu.SemaphoreType.DMA((2, lines)),
            pltpu.SemaphoreType.DMA((2, lines)),
        ],
        compiler_params=pltpu.CompilerParams(collective_id=0, has_side_effects=True),
    )(tokens, meta)


def replica_scatter(make_block, count):
    me = lax.axis_index("dp")
    upper, low = me // 2, me % 2
    pairs = [(i, i ^ 1) for i in range(count)]
    order = list(range(count // 2))[::-1]
    totals = {}
    for rel in order:
        dest = (upper ^ rel) * 2
        got = lax.ppermute(make_block(dest + 1 - low).astype(BF16), "dp", pairs)
        totals[rel] = make_block(dest + low) + got.astype(F32)
    bit = count // 4
    while bit:
        pairs = [(i, i ^ (2 * bit)) for i in range(count)]
        for rel in [r for r in totals if r & bit]:
            got = lax.ppermute(totals.pop(rel).astype(BF16), "dp", pairs)
            totals[rel ^ bit] = totals[rel ^ bit] + got.astype(F32)
        bit //= 2
    return totals[0].astype(BF16)


def block_of(array, count, index):
    size = array.shape[1] // count
    return lax.dynamic_slice_in_dim(array, index * size, size, 1)


def shards(tokens, grad_out, routes, combine, w_gate, w_up, w_down):
    tok_count, width = tokens.shape
    top_count = routes.shape[1]
    exp_local = w_gate.shape[0]
    owners = lax.axis_size("expert")
    replicas = lax.axis_size("dp")
    experts = exp_local * owners
    capacity = min(tok_count, 3 * tok_count * top_count // (2 * experts))
    slots = owners * capacity
    all_count = owners * tok_count
    first = lax.axis_index("expert") * exp_local
    lanes = -(-2 * experts // LANES) * LANES

    named = routes[:, :, None] == jnp.arange(experts, dtype=jnp.int32)[None, None, :]
    dense_weight = jnp.sum(jnp.where(named, combine.astype(F32)[:, :, None], 0.0), axis=1)
    dense_named = jnp.sum(named.astype(F32), axis=1)
    meta = jnp.concatenate([dense_named, dense_weight], axis=1).astype(BF16)
    meta = jnp.pad(meta, ((0, 0), (0, lanes - 2 * experts)))

    all_dy = lax.all_gather(grad_out, "expert", axis=0, tiled=True)
    all_x, all_meta = gather_pair(tokens, meta, owners)
    all_x = all_x.reshape(all_count, width)
    all_meta = all_meta.reshape(all_count, lanes)

    lane = jnp.arange(lanes, dtype=jnp.int32)[None, :]
    local_lane = first + jnp.arange(exp_local, dtype=jnp.int32)[:, None]
    mask = dot_tb((lane == local_lane).astype(BF16), all_meta)
    index = jnp.arange(all_count, dtype=jnp.int32)
    upto = (index[:, None] <= index[None, :]).astype(BF16)
    position = dot(mask.astype(BF16), upto).astype(jnp.int32) - 1
    position = jnp.where(mask > 0.5, position, -1)
    picks = (
        position[:, None, :] == jnp.arange(slots, dtype=jnp.int32)[None, :, None]
    ).astype(BF16)
    pick_all = picks.reshape(exp_local * slots, all_count)
    rows_meta = dot(pick_all, all_meta).reshape(exp_local, slots, lanes)
    weights = jnp.sum(
        jnp.where(lane[:, None, :] == experts + local_lane[:, :, None], rows_meta, 0.0),
        axis=2,
        keepdims=True,
    )
    forward = []
    for local in range(exp_local):
        rows_x = dot(picks[local], all_x).astype(BF16)
        pre_gate = dot(rows_x, w_gate[local])
        pre_up = dot(rows_x, w_up[local])
        forward.append((rows_x, pre_gate, pre_up))

    back_rows, gates, ups, downs = [], [], [], []
    for local in range(exp_local):
        rows_x, pre_gate, pre_up = forward[local]
        sigma = jax.nn.sigmoid(pre_gate)
        hidden = (pre_gate * sigma * pre_up).astype(BF16)
        rows_dy = dot(picks[local], all_dy).astype(BF16)
        scaled = (weights[local] * rows_dy.astype(F32)).astype(BF16)
        grad_hidden = dot_tb(scaled, w_down[local])
        grad_gate = (grad_hidden * pre_up * sigma * (1.0 + pre_gate * (1.0 - sigma))).astype(BF16)
        grad_up = (grad_hidden * pre_gate * sigma).astype(BF16)
        gates.append(
            replica_scatter(lambda j: dot_ta(block_of(rows_x, replicas, j), grad_gate), replicas)
        )
        ups.append(
            replica_scatter(lambda j: dot_ta(block_of(rows_x, replicas, j), grad_up), replicas)
        )
        downs.append(
            replica_scatter(lambda j: dot_ta(hidden, block_of(scaled, replicas, j)), replicas)
        )
        grad_rows = (dot_tb(grad_gate, w_gate[local]) + dot_tb(grad_up, w_up[local])).astype(BF16)
        output = dot(hidden, w_down[local])
        grad_weight = jnp.sum(rows_dy.astype(F32) * output, axis=-1, keepdims=True).astype(BF16)
        spread = jnp.where(lane == first + local, grad_weight, jnp.zeros((), BF16))
        back_rows.append(jnp.concatenate([grad_rows, spread], axis=1))
    back = dot_ta(pick_all, jnp.concatenate(back_rows, axis=0)).astype(BF16)
    back = lax.psum_scatter(back, "expert", scatter_dimension=0, tiled=True)
    grad_tokens = back[:, :width]
    spread = back[:, width : width + experts].astype(F32)
    grad_combine = jnp.sum(jnp.where(named, spread[:, None, :], 0.0), axis=2).astype(BF16)
    return (grad_tokens, grad_combine, jnp.stack(gates), jnp.stack(ups), jnp.stack(downs))


def solution(mesh):
    return jax.shard_map(
        shards,
        mesh=mesh,
        in_specs=(
            P(("dp", "expert"), None),
            P(("dp", "expert"), None),
            P(("dp", "expert"), None),
            P(("dp", "expert"), None),
            P("expert", None, None),
            P("expert", None, None),
            P("expert", None, None),
        ),
        out_specs=(
            P(("dp", "expert"), None),
            P(("dp", "expert"), None),
            P("expert", "dp", None),
            P("expert", "dp", None),
            P("expert", None, "dp"),
        ),
        check_vma=False,
    )
```

```python
import functools

import jax
import jax.numpy as jnp
from jax import lax
from jax.experimental import pallas as pl
from jax.experimental.pallas import tpu as pltpu
from jax.sharding import PartitionSpec as P

F32 = jnp.float32
BF16 = jnp.bfloat16
LANES = 128
MESH = pl.DeviceIdType.MESH


def dot(left, right):
    return jnp.dot(left, right, preferred_element_type=F32)


def dot_ta(left, right):
    return lax.dot_general(left, right, (((0,), (0,)), ((), ())), preferred_element_type=F32)


def dot_tb(left, right):
    return lax.dot_general(left, right, (((1,), (1,)), ((), ())), preferred_element_type=F32)


def gather_kernel(lines, x_ref, m_ref, ox_ref, om_ref, own, send_z, recv_z, send_y, recv_y):
    me = lax.axis_index("expert")
    line, side = me // 2, lax.rem(me, 2)
    across = line * 2 + 1 - side

    def peer(step):
        return lax.rem(line + step, lines) * 2 + side

    barrier = pltpu.get_barrier_semaphore()
    for step in range(1, lines):
        pl.semaphore_signal(barrier, inc=1, device_id={"expert": peer(step)}, device_id_type=MESH)
    pl.semaphore_signal(barrier, inc=1, device_id={"expert": across}, device_id_type=MESH)
    pl.semaphore_wait(barrier, lines)

    arrays = ((0, m_ref, om_ref), (1, x_ref, ox_ref))
    locals_, sends = [], []
    for which, src, dst in arrays:
        copy = pltpu.make_async_copy(src, dst.at[me], own.at[which])
        copy.start()
        locals_.append(copy)
        for step in range(1, lines):
            copy = pltpu.make_async_remote_copy(
                src_ref=src,
                dst_ref=dst.at[me],
                send_sem=send_z.at[which, step - 1],
                recv_sem=recv_z.at[which, step - 1],
                device_id={"expert": peer(step)},
                device_id_type=MESH,
            )
            copy.start()
            sends.append(copy)
        copy = pltpu.make_async_remote_copy(
            src_ref=src,
            dst_ref=dst.at[me],
            send_sem=send_y.at[which, 0],
            recv_sem=recv_y.at[which, 0],
            device_id={"expert": across},
            device_id_type=MESH,
        )
        copy.start()
        sends.append(copy)
    for which, src, dst in arrays:
        for step in sorted(range(1, lines), key=lambda s: min(s, lines - s)):
            origin = peer(lines - step)
            pltpu.make_async_remote_copy(
                src_ref=src,
                dst_ref=dst.at[origin],
                send_sem=send_z.at[which, step - 1],
                recv_sem=recv_z.at[which, step - 1],
                device_id={"expert": across},
                device_id_type=MESH,
            ).wait_recv()
            copy = pltpu.make_async_remote_copy(
                src_ref=dst.at[origin],
                dst_ref=dst.at[origin],
                send_sem=send_y.at[which, step],
                recv_sem=recv_y.at[which, step],
                device_id={"expert": across},
                device_id_type=MESH,
            )
            copy.start()
            sends.append(copy)
    for copy in locals_:
        copy.wait()
    for copy in sends:
        copy.wait_send()
    for which, src, dst in arrays:
        for step in range(lines):
            origin = lax.rem(line + lines - step, lines) * 2 + 1 - side
            pltpu.make_async_remote_copy(
                src_ref=src,
                dst_ref=dst.at[origin],
                send_sem=send_y.at[which, step],
                recv_sem=recv_y.at[which, step],
                device_id={"expert": across},
                device_id_type=MESH,
            ).wait_recv()


def gather_pair(tokens, meta, owners):
    lines = owners // 2
    anywhere = pl.BlockSpec(memory_space=pl.ANY)
    return pl.pallas_call(
        functools.partial(gather_kernel, lines),
        out_shape=(
            jax.ShapeDtypeStruct((owners,) + tokens.shape, tokens.dtype),
            jax.ShapeDtypeStruct((owners,) + meta.shape, meta.dtype),
        ),
        in_specs=[anywhere, anywhere],
        out_specs=(anywhere, anywhere),
        scratch_shapes=[
            pltpu.SemaphoreType.DMA((2,)),
            pltpu.SemaphoreType.DMA((2, lines - 1)),
            pltpu.SemaphoreType.DMA((2, lines - 1)),
            pltpu.SemaphoreType.DMA((2, lines)),
            pltpu.SemaphoreType.DMA((2, lines)),
        ],
        compiler_params=pltpu.CompilerParams(collective_id=0, has_side_effects=True),
    )(tokens, meta)


def replica_scatter(make_block, count, ready):
    me = lax.axis_index("dp")
    upper, low = me // 2, me % 2
    pairs = [(i, i ^ 1) for i in range(count)]
    order = list(range(count // 2))[::-1]
    totals = {}
    for rel in order:
        dest = (upper ^ rel) * 2
        got = lax.ppermute(make_block(dest + 1 - low).astype(BF16), "dp", pairs)
        totals[rel] = make_block(dest + low) + got.astype(F32)
    bit = count // 4
    while bit:
        pairs = [(i, i ^ (2 * bit)) for i in range(count)]
        for rel in [r for r in totals if r & bit]:
            sent = totals.pop(rel).astype(BF16)
            ready.append(sent)
            got = lax.ppermute(sent, "dp", pairs)
            totals[rel ^ bit] = totals[rel ^ bit] + got.astype(F32)
        bit //= 2
    return totals[0].astype(BF16)


def block_of(array, count, index):
    size = array.shape[1] // count
    return lax.dynamic_slice_in_dim(array, index * size, size, 1)


def shards(tokens, grad_out, routes, combine, w_gate, w_up, w_down):
    tok_count, width = tokens.shape
    top_count = routes.shape[1]
    exp_local = w_gate.shape[0]
    owners = lax.axis_size("expert")
    replicas = lax.axis_size("dp")
    experts = exp_local * owners
    capacity = min(tok_count, 3 * tok_count * top_count // (2 * experts))
    slots = owners * capacity
    all_count = owners * tok_count
    first = lax.axis_index("expert") * exp_local
    lanes = -(-2 * experts // LANES) * LANES

    named = routes[:, :, None] == jnp.arange(experts, dtype=jnp.int32)[None, None, :]
    dense_weight = jnp.sum(jnp.where(named, combine.astype(F32)[:, :, None], 0.0), axis=1)
    dense_named = jnp.sum(named.astype(F32), axis=1)
    meta = jnp.concatenate([dense_named, dense_weight], axis=1).astype(BF16)
    meta = jnp.pad(meta, ((0, 0), (0, lanes - 2 * experts)))

    all_dy = lax.all_gather(grad_out, "expert", axis=0, tiled=True)
    all_x, all_meta = gather_pair(tokens, meta, owners)
    all_x = all_x.reshape(all_count, width)
    all_meta = all_meta.reshape(all_count, lanes)

    lane = jnp.arange(lanes, dtype=jnp.int32)[None, :]
    local_lane = first + jnp.arange(exp_local, dtype=jnp.int32)[:, None]
    mask = dot_tb((lane == local_lane).astype(BF16), all_meta)
    index = jnp.arange(all_count, dtype=jnp.int32)
    upto = (index[:, None] <= index[None, :]).astype(BF16)
    position = dot(mask.astype(BF16), upto).astype(jnp.int32) - 1
    position = jnp.where(mask > 0.5, position, -1)
    picks = (
        position[:, None, :] == jnp.arange(slots, dtype=jnp.int32)[None, :, None]
    ).astype(BF16)
    pick_all = picks.reshape(exp_local * slots, all_count)
    rows_meta = dot(pick_all, all_meta).reshape(exp_local, slots, lanes)
    weights = jnp.sum(
        jnp.where(lane[:, None, :] == experts + local_lane[:, :, None], rows_meta, 0.0),
        axis=2,
        keepdims=True,
    )
    forward = []
    for local in range(exp_local):
        rows_x = dot(picks[local], all_x).astype(BF16)
        pre_gate = dot(rows_x, w_gate[local])
        pre_up = dot(rows_x, w_up[local])
        forward.append((rows_x, pre_gate, pre_up))

    back_rows, back_spread, gates, ups, downs = [], [], [], [], []
    for local in range(exp_local):
        rows_x, pre_gate, pre_up = forward[local]
        sigma = jax.nn.sigmoid(pre_gate)
        hidden = (pre_gate * sigma * pre_up).astype(BF16)
        rows_dy = dot(picks[local], all_dy).astype(BF16)
        ready = []
        scaled = (weights[local] * rows_dy.astype(F32)).astype(BF16)
        grad_hidden = dot_tb(scaled, w_down[local])
        grad_gate = (grad_hidden * pre_up * sigma * (1.0 + pre_gate * (1.0 - sigma))).astype(BF16)
        grad_up = (grad_hidden * pre_gate * sigma).astype(BF16)
        gates.append(
            replica_scatter(lambda j: dot_ta(block_of(rows_x, replicas, j), grad_gate), replicas, ready)
        )
        ups.append(
            replica_scatter(lambda j: dot_ta(block_of(rows_x, replicas, j), grad_up), replicas, ready)
        )
        downs.append(
            replica_scatter(lambda j: dot_ta(hidden, block_of(scaled, replicas, j)), replicas, [])
        )
        grad_rows = (dot_tb(grad_gate, w_gate[local]) + dot_tb(grad_up, w_up[local])).astype(BF16)
        output = dot(hidden, w_down[local])
        grad_weight = jnp.sum(rows_dy.astype(F32) * output, axis=-1, keepdims=True).astype(BF16)
        spread = jnp.where(lane == first + local, grad_weight, jnp.zeros((), BF16))
        back_rows.append(grad_rows)
        back_spread.append(spread)
        if local + 1 < exp_local:
            all_dy = lax.optimization_barrier((all_dy, *ready))[0]
    back = dot_ta(pick_all, jnp.concatenate(back_rows, axis=0)).astype(BF16)
    grad_tokens = lax.psum_scatter(back, "expert", scatter_dimension=0, tiled=True)
    spread = dot_ta(pick_all, jnp.concatenate(back_spread, axis=0)).astype(BF16)
    spread = lax.dynamic_slice_in_dim(spread, first, exp_local, 1)
    spread = lax.all_to_all(
        spread.reshape(owners, tok_count, exp_local), "expert", 0, 0, tiled=True
    )
    spread = spread.transpose(1, 0, 2).reshape(tok_count, experts).astype(F32)
    grad_combine = jnp.sum(jnp.where(named, spread[:, None, :], 0.0), axis=2).astype(BF16)
    return (grad_tokens, grad_combine, jnp.stack(gates), jnp.stack(ups), jnp.stack(downs))


def solution(mesh):
    return jax.shard_map(
        shards,
        mesh=mesh,
        in_specs=(
            P(("dp", "expert"), None),
            P(("dp", "expert"), None),
            P(("dp", "expert"), None),
            P(("dp", "expert"), None),
            P("expert", None, None),
            P("expert", None, None),
            P("expert", None, None),
        ),
        out_specs=(
            P(("dp", "expert"), None),
            P(("dp", "expert"), None),
            P("expert", "dp", None),
            P("expert", "dp", None),
            P("expert", None, "dp"),
        ),
        check_vma=False,
    )
```
